256 devices in a mesh: rep: 8 (over z_hi, core), wide: 32 (over z_lo, y, x).
Axes of the slice: x: 4, y: 4, z: 8 (z_hi: 4, z_lo: 2; z = z_hi * 2 + z_lo), core: 2. Of those that a mesh axis runs over, the one named last changes fastest.
Arguments:
- pool: bfloat16 [8192, 4096], P(('rep', 'wide')), may hold values from -6 to 6
- ids: int32 [6144], P('rep'), may hold values from 0 to 1023
- block_rows: int32 [2], replicated, may hold values from 0 to 15
- enc_weight: bfloat16 [4096, 32768], P(None, 'wide'), may hold values from -0.09375 to 0.09375
- enc_bias: float32 [32768], P('wide'), may hold values from -3 to 3
- dec_bias: float32 [4096], replicated, may hold values from -3 to 3
Outputs:
- gram: float32 [4096, 32768], P('rep', 'wide')
The draws below stay inside these ranges and needn't reach their ends.
All inputs are finite; a program needn't handle non-finite values.
Results may differ from the reference program's by a relative error of at most 0.0003.
Values may be sent and summed in bfloat16 or wider, within the bound.
A program may use at most 128 MiB of HBM per device.

```python
import jax
import jax.numpy as jnp
from jax import lax

D = 4096
LAT = 32768
BLOCK = 2048
NB = 2
TOK = 768
POOL = 1024
TOKENS = 6144
N_REP = 8


def plant(entries, own_key, low, top_value):
    place = [jax.random.randint(jax.random.fold_in(own_key, axis), (), 0, length) for axis, length in enumerate(entries.shape)]
    main_axis = entries.shape.index(max(entries.shape))
    next_to = place[:main_axis] + [(place[main_axis] + 1) % entries.shape[main_axis]] + place[main_axis + 1:]
    return entries.at[tuple(place)].set(low).at[tuple(next_to)].set(top_value)


def level_of(own_key, extent, cuts, low, top_value):
    def one(axis_at, shards_of):
        draws = jax.random.uniform(jax.random.fold_in(jax.random.fold_in(own_key, 6), axis_at), (shards_of,), jnp.float32, low / len(cuts), top_value / len(cuts))
        return jnp.repeat(jnp.exp(draws), extent[axis_at] // shards_of).reshape((-1,) + (1,) * (len(extent) - axis_at - 1))

    level = one(*cuts[0])
    for cut in cuts[1:]:
        level = level * one(*cut)
    return level


def gaussian(own_key, dims, scale, bound, pieces=(), kind=jnp.bfloat16):
    gain = level_of(own_key, dims, pieces, -0.22, 0.18) if pieces else 1.0
    drawn = jax.random.normal(own_key, dims, jnp.float32) * scale * gain
    return jnp.minimum(jnp.maximum(drawn, -bound), bound).astype(kind)


def setup_inputs(seed: int = 0) -> dict:
    streams_of = jax.random.split(jax.random.key(seed), 7)
    pool = gaussian(streams_of[0], (N_REP * POOL, D), 1.0, 6.0, ((0, 256),))
    ids = plant(jax.random.randint(streams_of[1], (TOKENS,), 0, POOL), jax.random.fold_in(streams_of[1], 1), 0, POOL - 1).astype(jnp.int32)
    block_rows = jax.random.randint(streams_of[2], (NB,), 0, LAT // BLOCK).astype(jnp.int32)
    enc_weight = gaussian(streams_of[3], (D, LAT), D ** -0.5, 0.09375, ((1, 32),))
    enc_bias = gaussian(streams_of[4], (LAT,), 0.5, 3.0, ((0, 32),), jnp.float32)
    dec_bias = gaussian(streams_of[5], (D,), 0.5, 3.0, (), jnp.float32)
    return {"pool": pool, "ids": ids, "block_rows": block_rows, "enc_weight": enc_weight, "enc_bias": enc_bias, "dec_bias": dec_bias}


def encode(rows, enc_weight, enc_bias, dec_bias):
    values = rows.astype(jnp.float32)
    power = lax.optimization_barrier(jnp.mean(values * values, axis=-1, keepdims=True))
    centered = (values * lax.rsqrt(power + 1e-06) - dec_bias).astype(jnp.bfloat16)
    before = jnp.dot(centered, enc_weight, preferred_element_type=jnp.float32) + enc_bias
    return jnp.maximum(before, 0.0).astype(jnp.bfloat16)

def reference(pool, ids, block_rows, enc_weight, enc_bias, dec_bias):
    columns = (block_rows[:, None] * BLOCK + jnp.arange(BLOCK, dtype=jnp.int32)[None, :]).reshape(-1).astype(jnp.int32)
    total = jnp.zeros((NB * BLOCK, LAT), jnp.float32)
    for replica in range(N_REP):
        table = pool[replica * POOL:(replica + 1) * POOL]
        picks = ids[replica * TOK:(replica + 1) * TOK].astype(jnp.int32)
        residual = jnp.take(table, picks, axis=0)
        codes = encode(residual, enc_weight, enc_bias, dec_bias)
        chosen = jnp.take(codes, columns, axis=1)
        partial_sum = lax.dot_general(chosen, codes, (((0,), (0,)), ((), ())), preferred_element_type=jnp.float32)
        total = total + partial_sum
    return total / float(TOK * N_REP)
```

```python
import functools

import jax
import jax.numpy as jnp
from jax import lax
from jax.experimental import pallas as pl
from jax.experimental.pallas import tpu as pltpu
from jax.sharding import PartitionSpec as P

BLOCK = 2048
D = 4096
TOK = 768
PANEL = 1024
HALF = 512
ROWS = 512
PIECE = 48
CHUNK = 192
MESH = pl.DeviceIdType.MESH
F32 = jnp.float32
BF16 = jnp.bfloat16


def kernel(pool_ref, pos_ref, rows_ref, w_hbm, eb_ref, db_ref, out_ref,
           w_vm, cent, pcodes, codes, a2a, sel, chosen,
           w_sem, ps, pr, cs, cr, as_, ar, rs, rr, zs, zr, fs, fr, ks, kr):
    r = lax.axis_index("rep")
    w = lax.axis_index("wide")
    h, c = r // 2, r % 2
    zl, y, x = w // 16, (w // 4) % 4, w % 4
    sends = []

    def wide_of(zz, yy, xx):
        return zz * 16 + yy * 4 + xx

    def copy(src, dst, ssem, rsem, dev):
        return pltpu.make_async_remote_copy(
            src_ref=src, dst_ref=dst, send_sem=ssem, recv_sem=rsem,
            device_id=dev, device_id_type=MESH)

    def send(src, dst, ssem, rsem, dev):
        d = copy(src, dst, ssem, rsem, dev)
        d.start()
        sends.append(d)

    def arrived(dst, ssem, rsem, dev):
        copy(dst, dst, ssem, rsem, dev).wait_recv()

    w_copy = pltpu.make_async_copy(w_hbm, w_vm, w_sem)
    w_copy.start()

    barrier = pltpu.get_barrier_semaphore()

    def greet_wide(i, carry):
        pl.semaphore_signal(barrier, inc=1, device_id=(r, (w + i) % 32), device_id_type=MESH)
        return carry

    def greet_rep(i, carry):
        pl.semaphore_signal(barrier, inc=1, device_id=((r + i) % 8, w), device_id_type=MESH)
        return carry

    lax.fori_loop(1, 32, greet_wide, 0)
    lax.fori_loop(1, 8, greet_rep, 0)

    for ab in range(2):
        values = pool_ref[ab * 16:(ab + 1) * 16, :].astype(F32)
        power = jnp.mean(values * values, axis=-1, keepdims=True)
        centered = (values * lax.rsqrt(power + 1e-06) - db_ref[...]).astype(BF16)
        if ab == 0:
            cent[0, y, zl, x] = centered
        else:
            cent[1, x, zl, y] = centered

    pl.semaphore_wait(barrier, 38)

    def gather(buf, ss, sr, own_ready, near_ready, far_ready):
        place = ((y, x), (x, y))

        def first(ab, d):
            if ab == 0:
                return (r, wide_of(zl, y, (x + d + 4) % 4))
            return (r, wide_of(zl, (y + d + 4) % 4, x))

        def second(ab, d):
            return first(1 - ab, d)

        other = (r, wide_of(1 - zl, y, x))
        steps = (1, -1)
        for ab in range(2):
            k, m = place[ab]
            own = buf.at[ab, k, zl, m]
            send(own, own, ss.at[ab, 0], sr.at[ab, 0], other)
            for i, d in enumerate(steps):
                send(own, own, ss.at[ab, 1 + i * 2 + zl], sr.at[ab, 1 + i * 2 + zl], first(ab, d))
        for ab in range(2):
            k, m = place[ab]
            got = buf.at[ab, k, 1 - zl, m]
            arrived(got, ss.at[ab, 0], sr.at[ab, 0], other)
            for i, d in enumerate(steps):
                s = 1 + i * 2 + 1 - zl
                send(got, got, ss.at[ab, s], sr.at[ab, s], first(ab, d))
        for ab in range(2):
            k, m = place[ab]
            for i, d in enumerate(steps):
                got = buf.at[ab, k, i, (m - d + 4) % 4]
                s = 1 + i * 2 + i
                arrived(got, ss.at[ab, s], sr.at[ab, s], first(ab, -d))
                send(got, got, ss.at[ab, 5 + i], sr.at[ab, 5 + i], first(ab, d))
        for ab in range(2):
            k, m = place[ab]
            for i, d in enumerate(steps):
                s = 1 + i * 2 + 1 - i
                arrived(buf.at[ab, k, 1 - i, (m - d + 4) % 4], ss.at[ab, s], sr.at[ab, s], first(ab, -d))
        for ab in range(2):
            k, m = place[ab]
            for i, d in enumerate(steps):
                arrived(buf.at[ab, k, i, (m + 2) % 4], ss.at[ab, 5 + i], sr.at[ab, 5 + i], first(ab, -d))
        for z in range(2):
            for ab in range(2):
                k, m = place[ab]
                for i, d in enumerate(steps):
                    part = buf.at[ab, k, z if i == 0 else 1 - z]
                    s = 7 + i * 2 + (z if i == 0 else 1 - z)
                    send(part, part, ss.at[ab, s], sr.at[ab, s], second(ab, d))
        own_ready()
        for ab in range(2):
            k, m = place[ab]
            for i, d in enumerate(steps):
                got = buf.at[ab, (k - d + 4) % 4, i]
                s = 7 + i * 2 + i
                arrived(got, ss.at[ab, s], sr.at[ab, s], second(ab, -d))
                send(got, got, ss.at[ab, 11 + i], sr.at[ab, 11 + i], second(ab, d))
        for i, d in enumerate(steps):
            for ab in range(2):
                k, m = place[ab]
                s = 7 + i * 2 + 1 - i
                arrived(buf.at[ab, (k - d + 4) % 4, 1 - i], ss.at[ab, s], sr.at[ab, s], second(ab, -d))
            near_ready(d)
        for ab in range(2):
            k, m = place[ab]
            for i, d in enumerate(steps):
                arrived(buf.at[ab, (k + 2) % 4, i], ss.at[ab, 11 + i], sr.at[ab, 11 + i], second(ab, -d))
        far_ready()

    def encode(ky, kx):
        def tile(n, carry):
            cols = pl.ds(pl.multiple_of(n * 256, 256), 256)
            lhs = jnp.concatenate(
                [cent[0, ky].reshape(128, D), cent[1, kx].reshape(128, D)], axis=0)
            before = jnp.dot(lhs, w_vm[:, cols], preferred_element_type=F32) + eb_ref[:, cols]
            made = jnp.maximum(before, 0.0).astype(BF16)
            pcodes[pl.ds(pl.multiple_of(ky * 128, 128), 128), cols] = made[:128]
            pcodes[pl.ds(pl.multiple_of(512 + kx * 128, 128), 128), cols] = made[128:]
            return carry

        lax.fori_loop(0, 4, tile, 0)

    def own_ready():
        w_copy.wait()
        encode(y, x)

    gather(cent, ps, pr, own_ready,
           lambda d: encode((y - d + 4) % 4, (x - d + 4) % 4),
           lambda: encode((y + 2) % 4, (x + 2) % 4))

    def pick(q, carry):
        rows = pl.ds(pl.multiple_of(q * CHUNK, CHUNK), CHUNK)
        hot = (pos_ref[rows, :] == lax.broadcasted_iota(jnp.int32, (CHUNK, 1024), 1)).astype(BF16)
        for half in range(2):
            got = jnp.dot(hot, pcodes[:, half * HALF:(half + 1) * HALF], preferred_element_type=F32)
            codes[r, half, rows, :] = got.astype(BF16)
        return carry

    lax.fori_loop(0, 4, pick, 0)

    def rep_of(d, core):
        return ((h + d + 4) % 4) * 2 + core

    def chunk(rep, q):
        return codes.at[rep, :, pl.ds(q * CHUNK, CHUNK), :]

    up, down = (rep_of(1, c), w), (rep_of(-1, c), w)
    twin = (rep_of(0, 1 - c), w)
    for q in range(4):
        send(chunk(r, q), chunk(r, q), zs.at[0, q], zr.at[0, q], up)
        p = (q + 2) % 4
        send(chunk(r, p), chunk(r, p), zs.at[1, p], zr.at[1, p], down)
    for q in range(4):
        send(chunk(r, q), chunk(r, q), ks.at[0, q], kr.at[0, q], twin)

    is_a = r < 4

    def part(j):
        zj, yj, xj = j // 16, (j // 4) % 4, j % 4
        xx, qc = xj // 2, xj % 2
        t = jnp.where(is_a, (yj * 2 + zj) * 2 + xx, (xx * 2 + zj) * 4 + yj)
        return codes.at[r, :, pl.ds(pl.multiple_of(t * PIECE, PIECE), PIECE),
                        pl.ds(pl.multiple_of(qc * 256, 256), 256)]

    def spread(i, carry):
        j = (w + i) % 32
        copy(part(j), a2a.at[w], as_.at[i], ar.at[i], (r, j)).start()
        return carry

    lax.fori_loop(1, 32, spread, 0)
    mine = pltpu.make_async_copy(part(w), a2a.at[w], as_.at[0])
    mine.start()
    mine.wait()

    def collect(i, carry):
        j = (w - i + 32) % 32
        arrived(a2a.at[j], as_.at[i], ar.at[i], (r, j))
        return carry

    lax.fori_loop(1, 32, collect, 0)

    my_k = jnp.where(is_a, y, x)
    my_m = jnp.where(is_a, x, y)
    my_ab = r // 4
    for i in range(8):
        rd = (r + i) % 8
        hd, cd = rd // 2, rd % 2
        owner = rows_ref[hd // 2] * 2 + hd % 2
        got = a2a[owner, cd]
        dst = chosen.at[my_ab, my_k, zl, my_m, r % 4]
        if i == 0:
            dst[...] = got
        else:
            sel[i] = got
            send(sel.at[i], dst, rs.at[i], rr.at[i], (rd, w))
    for i in range(1, 8):
        src = (r - i + 8) % 8
        s_a = src < 4
        dst = chosen.at[src // 4, jnp.where(s_a, y, x), zl, jnp.where(s_a, x, y), src % 4]
        arrived(dst, rs.at[i], rr.at[i], (src, w))

    nothing = lambda *a: None
    gather(chosen, cs, cr, nothing, nothing, nothing)

    def gram(rep, first=False):
        ab, slot = rep // 4, rep % 4
        in_a = ab == 0

        def quarter(qc, carry):
            parts = []
            for t in range(16):
                k = jnp.where(in_a, t // 4, 2 * (t // 8) + qc)
                z = jnp.where(in_a, (t // 2) % 2, (t // 4) % 2)
                m = jnp.where(in_a, 2 * (t % 2) + qc, t % 4)
                parts.append(chosen[ab, k, z, m, slot])
            lhs = jnp.concatenate(parts, axis=0)
            at = pl.ds(pl.multiple_of(qc * 256, 256), 256)
            for half in range(2):
                made = lax.dot_general(lhs, codes[rep, half], (((0,), (0,)), ((), ())),
                                       preferred_element_type=F32)
                cols = slice(half * HALF, (half + 1) * HALF)
                if first:
                    out_ref[at, cols] = made
                else:
                    out_ref[at, cols] += made
            return carry

        lax.fori_loop(0, 2, quarter, 0)

    def twin_arrived(k, q):
        got = chunk(rep_of((0, -1, 1, 2)[k], 1 - c), q)
        arrived(got, ks.at[k, q], kr.at[k, q], twin)

    def to_twin(k, q):
        part_ = chunk(rep_of((0, -1, 1, 2)[k], c), q)
        send(part_, part_, ks.at[k, q], kr.at[k, q], twin)

    gram(r, first=True)
    for q in range(4):
        got = chunk(rep_of(-1, c), q)
        arrived(got, zs.at[0, q], zr.at[0, q], down)
        if q < 2:
            send(got, got, fs.at[0, q], fr.at[0, q], up)
        to_twin(1, q)
        p = (q + 2) % 4
        got = chunk(rep_of(1, c), p)
        arrived(got, zs.at[1, p], zr.at[1, p], up)
        if q < 2:
            send(got, got, fs.at[1, q], fr.at[1, q], down)
        to_twin(2, p)
    for q in range(4):
        twin_arrived(0, q)
    gram(rep_of(0, 1 - c))
    for k, d in ((1, -1), (2, 1)):
        gram(rep_of(d, c))
        for q in range(4):
            twin_arrived(k, q)
        gram(rep_of(d, 1 - c))
    for q in range(2):
        arrived(chunk(rep_of(2, c), q), fs.at[0, q], fr.at[0, q], down)
        to_twin(3, q)
        arrived(chunk(rep_of(2, c), q + 2), fs.at[1, q], fr.at[1, q], up)
        to_twin(3, q + 2)
    gram(rep_of(2, c))
    for q in range(4):
        twin_arrived(3, q)
    gram(rep_of(2, 1 - c))
    out_ref[...] = out_ref[...] * (1.0 / 6144.0)

    for d in sends:
        d.wait_send()

    def sent(i, carry):
        j = (w + i) % 32
        copy(part(j), a2a.at[w], as_.at[i], ar.at[i], (r, j)).wait_send()
        return carry

    lax.fori_loop(1, 32, sent, 0)


def local(pool, ids, block_rows, enc_weight, enc_bias, dec_bias):
    ab, j, wp = (ids % 32) // 16, ids % 16, ids // 32
    zl, y, x = wp // 16, (wp // 4) % 4, wp % 4
    k = jnp.where(ab == 0, y, x)
    m = jnp.where(ab == 0, x, y)
    pos = (ab * 512 + k * 128 + zl * 64 + m * 16 + j).reshape(TOK, 1)
    vmem = pl.BlockSpec(memory_space=pltpu.VMEM)
    smem = pl.BlockSpec(memory_space=pltpu.SMEM)
    dma = pltpu.SemaphoreType.DMA
    return pl.pallas_call(
        kernel,
        out_shape=jax.ShapeDtypeStruct((ROWS, PANEL), F32),
        in_specs=[vmem, vmem, smem, pl.BlockSpec(memory_space=pl.ANY), vmem, vmem],
        out_specs=vmem,
        scratch_shapes=[
            pltpu.VMEM((D, PANEL), BF16),
            pltpu.VMEM((2, 4, 2, 4, 16, D), BF16),
            pltpu.VMEM((1024, PANEL), BF16),
            pltpu.VMEM((8, 2, TOK, HALF), BF16),
            pltpu.VMEM((32, 2, PIECE, 256), BF16),
            pltpu.VMEM((8, PIECE, 256), BF16),
            pltpu.VMEM((2, 4, 2, 4, 4, PIECE, 256), BF16),
            dma,
            dma((2, 13)), dma((2, 13)),
            dma((2, 13)), dma((2, 13)),
            dma((32,)), dma((32,)),
            dma((8,)), dma((8,)),
            dma((2, 4)), dma((2, 4)),
            dma((2, 2)), dma((2, 2)),
            dma((4, 4)), dma((4, 4)),
        ],
        compiler_params=pltpu.CompilerParams(
            collective_id=0, has_side_effects=True, vmem_limit_bytes=58 * 1024 * 1024),
    )(pool, pos, block_rows, enc_weight, enc_bias.reshape(1, PANEL), dec_bias.reshape(1, D))


def solution(mesh):
    placed = (P(("rep", "wide"), None), P("rep"), P(), P(None, "wide"), P("wide"), P())
    return jax.shard_map(
        local, mesh=mesh, in_specs=placed, out_specs=P("rep", "wide"), check_vma=False
    )
```

```python
import functools

import jax
import jax.numpy as jnp
from jax import lax
from jax.experimental import pallas as pl
from jax.experimental.pallas import tpu as pltpu
from jax.sharding import PartitionSpec as P

BLOCK = 2048
D = 4096
TOK = 768
PANEL = 1024
HALF = 512
ROWS = 512
PIECE = 48
CHUNK = 192
MESH = pl.DeviceIdType.MESH
F32 = jnp.float32
BF16 = jnp.bfloat16


def kernel(pool_ref, pos_ref, rows_ref, w_hbm, eb_ref, db_ref, out_ref,
           w_vm, cent, pcodes, codes, ybuf, xsend, xbuf, zsend, zbuf, sel, chosen,
           w_sem, go, l_sem, ps, pr, cs, cr, ys, yr, xs, xr, qs, qr, rs, rr, zs, zr, fs, fr, ks, kr):
    r = lax.axis_index("rep")
    w = lax.axis_index("wide")
    h, core = r // 2, r % 2
    zl, y, x = w // 16, (w // 4) % 4, w % 4

    def wide_of(zz, yy, xx):
        return zz * 16 + yy * 4 + xx

    w_copy = pltpu.make_async_copy(w_hbm, w_vm, w_sem)
    w_copy.start()

    barrier = pltpu.get_barrier_semaphore()
    partners = [((r + i) % 8, w) for i in range(1, 8)]
    partners += [(r, wide_of(zl, (y + i) % 4, x)) for i in range(1, 4)]
    partners += [(r, wide_of(zl, y, (x + i) % 4)) for i in range(1, 4)]
    partners += [((r + i) % 8, wide_of(1 - zl, y, x)) for i in range(8)]
    for device in partners:
        pl.semaphore_signal(barrier, inc=1, device_id=device, device_id_type=MESH)

    for ab in range(2):
        values = pool_ref[ab * 16:(ab + 1) * 16, :].astype(F32)
        power = jnp.mean(values * values, axis=-1, keepdims=True)
        centered = (values * lax.rsqrt(power + 1e-06) - db_ref[...]).astype(BF16)
        if ab == 0:
            cent[0, y, zl, x] = centered
        else:
            cent[1, x, zl, y] = centered

    pl.semaphore_wait(barrier, len(partners))

    def program(c):
        sends = []
        twin = (h * 2 + 1 - c, w)
        other = (r, wide_of(1 - zl, y, x))

        def copy(src, dst, ssem, rsem, dev):
            return pltpu.make_async_remote_copy(
                src_ref=src, dst_ref=dst, send_sem=ssem, recv_sem=rsem,
                device_id=dev, device_id_type=MESH)

        def send(src, dst, ssem, rsem, dev):
            d = copy(src, dst, ssem, rsem, dev)
            d.start()
            sends.append(d)

        def arrived(dst, ssem, rsem, dev):
            copy(dst, dst, ssem, rsem, dev).wait_recv()

        place = ((y, x), (x, y))
        steps = (1, -1)

        def first(ab, d):
            if ab == 0:
                return (r, wide_of(zl, y, (x + d + 4) % 4))
            return (r, wide_of(zl, (y + d + 4) % 4, x))

        def second(ab, d):
            return first(1 - ab, d)

        def gather_rows(hold):
            def piece(ab, dk, e, dm):
                k, m = place[ab]
                return cent.at[ab, (k + dk + 4) % 4, zl if e == 0 else 1 - zl, (m + dm + 4) % 4]

            def got(ab, at, s, dev):
                arrived(at, ps.at[ab, s], pr.at[ab, s], dev)

            def put(ab, at, s, dev):
                send(at, at, ps.at[ab, s], pr.at[ab, s], dev)

            held = []

            def across(ab, e, dm):
                def go_across():
                    for i, d in enumerate(steps):
                        put(ab, piece(ab, 0, e, dm), 7 + i * 8 + e * 4 + dm % 4, second(ab, d))
                held.append(go_across)
                if hold is None:
                    held.pop()()

            for ab in range(2):
                put(ab, piece(ab, 0, 0, 0), 0, other)
                for i, d in enumerate(steps):
                    put(ab, piece(ab, 0, 0, 0), 1 + i * 2, first(ab, d))
                across(ab, 0, 0)
            for ab in range(2):
                got(ab, piece(ab, 0, 1, 0), 0, other)
                for i, d in enumerate(steps):
                    put(ab, piece(ab, 0, 1, 0), 2 + i * 2, first(ab, d))
                across(ab, 1, 0)
            for e in range(2):
                for i, d in ((0, 1), (1, -1)):
                    for ab in range(2):
                        got(ab, piece(ab, 0, e, -d), 1 + i * 2 + e, first(ab, -d))
                        if e == i:
                            put(ab, piece(ab, 0, e, -d), 5 + i, first(ab, d))
                        across(ab, e, -d)
            for i, d in enumerate(steps):
                for ab in range(2):
                    got(ab, piece(ab, 0, i, 2), 5 + i, first(ab, -d))
                    across(ab, i, 2)
            if hold is not None:
                hold()
                for task in held:
                    task()
            yield 3
            order = (0, -1, 1, 2)
            for dm in order:
                for ab in range(2):
                    for i, d in enumerate(steps):
                        s = 7 + i * 8 + i * 4 + dm % 4
                        got(ab, piece(ab, -d, i, dm), s, second(ab, -d))
                        put(ab, piece(ab, -d, i, dm), 23 + i * 4 + dm % 4, second(ab, d))
            for i, d in enumerate(steps):
                for ab in range(2):
                    for dm in order:
                        got(ab, piece(ab, -d, 1 - i, dm), 7 + i * 8 + (1 - i) * 4 + dm % 4, second(ab, -d))
                yield 5 + i
            for ab in range(2):
                for i, d in enumerate(steps):
                    for dm in order:
                        got(ab, piece(ab, 2, i, dm), 23 + i * 4 + dm % 4, second(ab, -d))
            yield 7

        def gather_chosen(par):
            ss, sr = cs.at[par], cr.at[par]

            def move(ab, at, s, dev):
                send(at, at, ss.at[ab, s], sr.at[ab, s], dev)

            def got(ab, at, s, dev):
                arrived(at, ss.at[ab, s], sr.at[ab, s], dev)

            for ab in range(2):
                k, m = place[ab]
                for i, d in enumerate(steps):
                    move(ab, chosen.at[par, ab, k, m], i, first(ab, d))
            yield 0
            for ab in range(2):
                k, m = place[ab]
                for i, d in enumerate(steps):
                    at = chosen.at[par, ab, k, (m - d + 4) % 4]
                    got(ab, at, i, first(ab, -d))
                    move(ab, chosen.at[par, ab, k, (m - d + 4) % 4, i], 2 + i, first(ab, d))
            yield 1
            for ab in range(2):
                k, m = place[ab]
                for i, d in enumerate(steps):
                    got(ab, chosen.at[par, ab, k, (m + 2) % 4, i], 2 + i, first(ab, -d))
                for i, d in enumerate(steps):
                    move(ab, chosen.at[par, ab, k], 4 + i, second(ab, d))
            yield 2
            for ab in range(2):
                k, m = place[ab]
                for i, d in enumerate(steps):
                    kk = (k - d + 4) % 4
                    got(ab, chosen.at[par, ab, kk], 4 + i, second(ab, -d))
                    move(ab, chosen.at[par, ab, kk, pl.ds(2 * i, 2)], 6 + i, second(ab, d))
            yield 3
            for ab in range(2):
                k, m = place[ab]
                for i, d in enumerate(steps):
                    got(ab, chosen.at[par, ab, (k + 2) % 4, pl.ds(2 * i, 2)], 6 + i, second(ab, -d))
            yield 4

        def until(task, mark):
            while next(task) != mark:
                pass

        def encode(d):
            ky, kx = (y + d + 4) % 4, (x + d + 4) % 4

            def tile(n, carry):
                cols = pl.ds(pl.multiple_of(n * 256, 256), 256)
                lhs = jnp.concatenate(
                    [cent[0, ky].reshape(128, D), cent[1, kx].reshape(128, D)], axis=0)
                before = jnp.dot(lhs, w_vm[:, cols], preferred_element_type=F32) + eb_ref[:, cols]
                made = jnp.maximum(before, 0.0).astype(BF16)
                pcodes[pl.ds(pl.multiple_of(ky * 128, 128), 128), cols] = made[:128]
                pcodes[pl.ds(pl.multiple_of(512 + kx * 128, 128), 128), cols] = made[128:]
                return carry

            lax.fori_loop(0, 4, tile, 0)

        rows = gather_rows(None if c == 0 else lambda: pl.semaphore_wait(go, 1))
        until(rows, 3)
        w_copy.wait()
        encode(0)
        until(rows, 5)
        encode(-1)
        until(rows, 6)
        encode(1)
        until(rows, 7)
        if c == 0:
            pl.semaphore_signal(go, inc=1, device_id=twin, device_id_type=MESH)
        encode(2)

        def pick(q, carry):
            at = pl.ds(pl.multiple_of(q * CHUNK, CHUNK), CHUNK)
            hot = (pos_ref[at, :] == lax.broadcasted_iota(jnp.int32, (CHUNK, 1024), 1)).astype(BF16)
            for half in range(2):
                got = jnp.dot(hot, pcodes[:, half * HALF:(half + 1) * HALF], preferred_element_type=F32)
                codes[r, half, at, :] = got.astype(BF16)
            return carry

        lax.fori_loop(0, 4, pick, 0)

        def rep_of(d, core_):
            return ((h + d + 4) % 4) * 2 + core_

        def chunk(rep, q):
            return codes.at[rep, :, pl.ds(q * CHUNK, CHUNK), :]

        up, down = (rep_of(1, c), w), (rep_of(-1, c), w)

        def along_z(q):
            send(chunk(r, q), chunk(r, q), zs.at[0, q], zr.at[0, q], up)
            p = (q + 2) % 4
            send(chunk(r, p), chunk(r, p), zs.at[1, p], zr.at[1, p], down)

        def to_twin(k, q):
            part = chunk(rep_of((0, -1, 1, 2)[k], c), q)
            send(part, part, ks.at[k, q], kr.at[k, q], twin)

        def twin_arrived(k):
            for q in range(4):
                arrived(chunk(rep_of((0, -1, 1, 2)[k], 1 - c), q), ks.at[k, q], kr.at[k, q], twin)

        def pass_on(q):
            got = chunk(rep_of(-1, c), q)
            arrived(got, zs.at[0, q], zr.at[0, q], down)
            if q < 2:
                send(got, got, fs.at[0, q], fr.at[0, q], up)
            to_twin(1, q)
            p = (q + 2) % 4
            got = chunk(rep_of(1, c), p)
            arrived(got, zs.at[1, p], zr.at[1, p], up)
            if q < 2:
                send(got, got, fs.at[1, q], fr.at[1, q], down)
            to_twin(2, p)

        def far_codes():
            for q in range(2):
                arrived(chunk(rep_of(2, c), q), fs.at[0, q], fr.at[0, q], down)
                to_twin(3, q)
                arrived(chunk(rep_of(2, c), q + 2), fs.at[1, q], fr.at[1, q], up)
                to_twin(3, q + 2)

        def owner(k, p):
            return rows_ref[k] * 2 + p

        def route():
            for i in range(1, 4):
                yy = (y + i) % 4
                part = codes.at[r, :, pl.ds(pl.multiple_of(yy * CHUNK, CHUNK), CHUNK), :]
                send(part, ybuf.at[y], ys.at[i], yr.at[i], (r, wide_of(zl, yy, x)))
            mine = pltpu.make_async_copy(
                codes.at[r, :, pl.ds(pl.multiple_of(y * CHUNK, CHUNK), CHUNK), :], ybuf.at[y], l_sem)
            mine.start()
            yield 0
            mine.wait()
            for i in range(1, 4):
                src = (y - i + 4) % 4
                arrived(ybuf.at[src], ys.at[i], yr.at[i], (r, wide_of(zl, src, x)))
            for k in range(2):
                xsend[k] = ybuf[(owner(k, x % 2) // 4) % 4]
            for i in range(1, 4):
                xx = (x + i) % 4
                part = xsend.at[:, :, pl.ds(pl.multiple_of(xx * PIECE, PIECE), PIECE), :]
                send(part, xbuf.at[x], xs.at[i], xr.at[i], (r, wide_of(zl, y, xx)))
            xbuf[x] = xsend[:, :, pl.ds(pl.multiple_of(x * PIECE, PIECE), PIECE), :]
            yield 1
            for i in range(1, 4):
                src = (x - i + 4) % 4
                arrived(xbuf.at[src], xs.at[i], xr.at[i], (r, wide_of(zl, y, src)))
            for hd in range(4):
                k, p = hd // 2, hd % 2
                xo = owner(k, p) % 4
                zsend[hd] = xbuf[xo, k, :, :, pl.ds(pl.multiple_of((1 - zl) * 256, 256), 256)]
                zbuf[zl, hd] = xbuf[xo, k, :, :, pl.ds(pl.multiple_of(zl * 256, 256), 256)]
            send(zsend, zbuf.at[zl], qs, qr, other)
            yield 2
            arrived(zbuf.at[1 - zl], qs, qr, other)
            ab = h // 2
            place_k = jnp.where(ab == 0, y, x)
            place_m = jnp.where(ab == 0, x, y)
            dst = chosen.at[c, ab, place_k, place_m, zl, h % 2]
            for i in (4, 3, 5, 2, 6, 1, 7, 0):
                rd = (r + i) % 8
                hd, cd = rd // 2, (c + i) % 2
                sel[i] = zbuf[owner(hd // 2, hd % 2) // 16, hd, cd]
                if i == 0:
                    dst[...] = sel[i]
                else:
                    send(sel.at[i], dst, rs.at[0, i], rr.at[0, i], (rd, w))
                send(sel.at[i], dst, rs.at[1, i], rr.at[1, i], (rd, other[1]))
            yield 3

        def pieces_arrived(par):
            for i in range(8):
                if (c - i) % 2 != par:
                    continue
                src = (r - i + 8) % 8
                hs = src // 2
                ab = hs // 2
                at = (par, ab, jnp.where(ab == 0, y, x), jnp.where(ab == 0, x, y))
                if i > 0:
                    arrived(chosen.at[at + (zl, hs % 2)], rs.at[0, i], rr.at[0, i], (src, w))
                arrived(chosen.at[at + (1 - zl, hs % 2)], rs.at[1, i], rr.at[1, i], (src, other[1]))

        def gram(d, par, first=False):
            hs = (h + d + 4) % 4
            ab, slot = hs // 2, hs % 2
            rep = hs * 2 + par

            def quarter(qc, carry):
                parts = []
                for t in range(16):
                    k = jnp.where(ab == 0, t // 4, t % 4)
                    m = jnp.where(ab == 0, t % 4, t // 4)
                    parts.append(chosen[par, ab, k, m, qc, slot])
                lhs = jnp.concatenate(parts, axis=0)
                at = pl.ds(pl.multiple_of(qc * 256, 256), 256)
                for half in range(2):
                    made = lax.dot_general(lhs, codes[rep, half], (((0,), (0,)), ((), ())),
                                           preferred_element_type=F32)
                    cols = slice(half * HALF, (half + 1) * HALF)
                    if first:
                        out_ref[at, cols] = made
                    else:
                        out_ref[at, cols] += made
                return carry

            lax.fori_loop(0, 2, quarter, 0)

        deal = route()
        spread = [gather_chosen(par) for par in range(2)]
        until(deal, 0)
        if c == 0:
            along_z(0)
            along_z(1)
            along_z(2)
            for q in range(4):
                to_twin(0, q)
            until(deal, 1)
            until(deal, 2)
            until(deal, 3)
            along_z(3)
            pass_on(0)
            pass_on(1)
            pieces_arrived(0)
            until(spread[0], 2)
            pass_on(2)
            pass_on(3)
            until(spread[0], 4)
            gram(0, 0, first=True)
            gram(-1, 0)
            gram(1, 0)
            pieces_arrived(1)
            until(spread[1], 2)
            far_codes()
            until(spread[1], 4)
            gram(2, 0)
            for k, d in enumerate((0, -1, 1, 2)):
                twin_arrived(k)
                gram(d, 1)
        else:
            along_z(0)
            along_z(1)
            for q in range(4):
                to_twin(0, q)
            pieces_arrived(0)
            until(spread[0], 1)
            until(deal, 1)
            until(spread[0], 2)
            until(deal, 2)
            until(deal, 3)
            along_z(2)
            along_z(3)
            pass_on(0)
            pass_on(1)
            until(spread[0], 4)
            pieces_arrived(1)
            until(spread[1], 2)
            pass_on(2)
            pass_on(3)
            until(spread[1], 4)
            twin_arrived(0)
            gram(0, 0, first=True)
            gram(0, 1)
            for k, d in ((1, -1), (2, 1)):
                twin_arrived(k)
                gram(d, 0)
                gram(d, 1)
            twin_arrived(3)
            gram(2, 0)
            far_codes()
            gram(2, 1)

        for d in sends:
            d.wait_send()

    @pl.when(core == 0)
    def _():
        program(0)

    @pl.when(core == 1)
    def _():
        program(1)


def local(pool, ids, block_rows, enc_weight, enc_bias, dec_bias):
    ab, j, wp = (ids % 32) // 16, ids % 16, ids // 32
    zl, y, x = wp // 16, (wp // 4) % 4, wp % 4
    k = jnp.where(ab == 0, y, x)
    m = jnp.where(ab == 0, x, y)
    pos = (ab * 512 + k * 128 + zl * 64 + m * 16 + j).reshape(TOK, 1)
    vmem = pl.BlockSpec(memory_space=pltpu.VMEM)
    smem = pl.BlockSpec(memory_space=pltpu.SMEM)
    dma = pltpu.SemaphoreType.DMA
    summed = pl.pallas_call(
        kernel,
        out_shape=jax.ShapeDtypeStruct((ROWS, PANEL), F32),
        in_specs=[vmem, vmem, smem, pl.BlockSpec(memory_space=pl.ANY), vmem, vmem],
        out_specs=vmem,
        scratch_shapes=[
            pltpu.VMEM((D, PANEL), BF16),
            pltpu.VMEM((2, 4, 2, 4, 16, D), BF16),
            pltpu.VMEM((1024, PANEL), BF16),
            pltpu.VMEM((8, 2, TOK, HALF), BF16),
            pltpu.VMEM((4, 2, CHUNK, HALF), BF16),
            pltpu.VMEM((2, 2, CHUNK, HALF), BF16),
            pltpu.VMEM((4, 2, 2, PIECE, HALF), BF16),
            pltpu.VMEM((4, 2, PIECE, 256), BF16),
            pltpu.VMEM((2, 4, 2, PIECE, 256), BF16),
            pltpu.VMEM((8, PIECE, 256), BF16),
            pltpu.VMEM((2, 2, 4, 4, 2, 2, PIECE, 256), BF16),
            dma, pltpu.SemaphoreType.REGULAR, dma,
            dma((2, 31)), dma((2, 31)),
            dma((2, 2, 8)), dma((2, 2, 8)),
            dma((4,)), dma((4,)),
            dma((4,)), dma((4,)),
            dma, dma,
            dma((2, 8)), dma((2, 8)),
            dma((2, 4)), dma((2, 4)),
            dma((2, 2)), dma((2, 2)),
            dma((4, 4)), dma((4, 4)),
        ],
        compiler_params=pltpu.CompilerParams(
            collective_id=0, has_side_effects=True, vmem_limit_bytes=58 * 1024 * 1024),
    )(pool, pos, block_rows, enc_weight, enc_bias.reshape(1, PANEL), dec_bias.reshape(1, D))
    return summed * (1.0 / 6144.0)


def solution(mesh):
    placed = (P(("rep", "wide"), None), P("rep"), P(), P(None, "wide"), P("wide"), P())
    return jax.shard_map(
        local, mesh=mesh, in_specs=placed, out_specs=P("rep", "wide"), check_vma=False
    )
```

```python
import jax
import jax.numpy as jnp
from jax import lax
from jax.experimental import pallas as pl
from jax.experimental.pallas import tpu as pltpu
from jax.sharding import PartitionSpec as P

BLOCK = 2048
D = 4096
TOK = 768
PANEL = 1024
HALF = 512
ROWS = 512
PIECE = 48
CHUNK = 192
MESH = pl.DeviceIdType.MESH
F32 = jnp.float32
BF16 = jnp.bfloat16


def kernel(pool_ref, ids_ref, rows_ref, w_hbm, eb_ref, db_ref, out_ref,
           pos_ref, w_vm, cent, pcodes, codes, ybuf, xsend, xbuf, zsend, zbuf, sel, chosen,
           w_sem, go, l_sem, ps, pr, cs, cr, ys, yr, xs, xr, qs, qr, rs, rr, zs, zr, fs, fr, ks, kr):
    r = lax.axis_index("rep")
    w = lax.axis_index("wide")
    h, core = r // 2, r % 2
    zl, y, x = w // 16, (w // 4) % 4, w % 4

    def wide_of(zz, yy, xx):
        return zz * 16 + yy * 4 + xx

    w_copy = pltpu.make_async_copy(w_hbm, w_vm, w_sem)
    w_copy.start()

    barrier = pltpu.get_barrier_semaphore()
    partners = [((r + i) % 8, w) for i in range(1, 8)]
    partners += [(r, wide_of(zl, (y + i) % 4, x)) for i in range(1, 4)]
    partners += [(r, wide_of(zl, y, (x + i) % 4)) for i in range(1, 4)]
    partners += [((r + i) % 8, wide_of(1 - zl, y, x)) for i in range(8)]
    for device in partners:
        pl.semaphore_signal(barrier, inc=1, device_id=device, device_id_type=MESH)

    for ab in range(2):
        values = pool_ref[ab * 16:(ab + 1) * 16, :].astype(F32)
        power = jnp.mean(values * values, axis=-1, keepdims=True)
        centered = (values * lax.rsqrt(power + 1e-06) - db_ref[...]).astype(BF16)
        if ab == 0:
            cent[0, y, zl, x] = centered
        else:
            cent[1, x, zl, y] = centered

    for n in range(TOK // 128):
        ids = ids_ref[n * 128:(n + 1) * 128].reshape(1, 128)
        ab, wp = (ids // 16) % 2, ids // 32
        z_, y_, x_ = wp // 16, (wp // 4) % 4, wp % 4
        k_ = jnp.where(ab == 0, y_, x_)
        m_ = jnp.where(ab == 0, x_, y_)
        place = ab * 512 + k_ * 128 + z_ * 64 + m_ * 16 + ids % 16
        pos_ref[n * 128:(n + 1) * 128, :] = jnp.broadcast_to(place, (128, 128)).T

    pl.semaphore_wait(barrier, len(partners))

    def program(c):
        sends = []
        twin = (h * 2 + 1 - c, w)
        other = (r, wide_of(1 - zl, y, x))

        def copy(src, dst, ssem, rsem, dev):
            return pltpu.make_async_remote_copy(
                src_ref=src, dst_ref=dst, send_sem=ssem, recv_sem=rsem,
                device_id=dev, device_id_type=MESH)

        def send(src, dst, ssem, rsem, dev):
            d = copy(src, dst, ssem, rsem, dev)
            d.start()
            sends.append(d)

        def arrived(dst, ssem, rsem, dev):
            copy(dst, dst, ssem, rsem, dev).wait_recv()

        place = ((y, x), (x, y))
        steps = (1, -1)

        def first(ab, d):
            if ab == 0:
                return (r, wide_of(zl, y, (x + d + 4) % 4))
            return (r, wide_of(zl, (y + d + 4) % 4, x))

        def second(ab, d):
            return first(1 - ab, d)

        def gather_rows(hold):
            def piece(ab, dk, e, dm):
                k, m = place[ab]
                return cent.at[ab, (k + dk + 4) % 4, zl if e == 0 else 1 - zl, (m + dm + 4) % 4]

            def got(ab, at, s, dev):
                arrived(at, ps.at[ab, s], pr.at[ab, s], dev)

            def put(ab, at, s, dev):
                send(at, at, ps.at[ab, s], pr.at[ab, s], dev)

            if hold is not None:
                hold()

            def across(ab, e, dm):
                for i, d in enumerate(steps):
                    put(ab, piece(ab, 0, e, dm), 7 + i * 8 + e * 4 + dm % 4, second(ab, d))

            for ab in range(2):
                put(ab, piece(ab, 0, 0, 0), 0, other)
                for i, d in enumerate(steps):
                    put(ab, piece(ab, 0, 0, 0), 1 + i * 2, first(ab, d))
                across(ab, 0, 0)
            for ab in range(2):
                got(ab, piece(ab, 0, 1, 0), 0, other)
                for i, d in enumerate(steps):
                    put(ab, piece(ab, 0, 1, 0), 2 + i * 2, first(ab, d))
                across(ab, 1, 0)
            for e in range(2):
                for i, d in ((0, 1), (1, -1)):
                    for ab in range(2):
                        got(ab, piece(ab, 0, e, -d), 1 + i * 2 + e, first(ab, -d))
                        if e == i:
                            put(ab, piece(ab, 0, e, -d), 5 + i, first(ab, d))
                        across(ab, e, -d)
            for i, d in enumerate(steps):
                for ab in range(2):
                    got(ab, piece(ab, 0, i, 2), 5 + i, first(ab, -d))
                    across(ab, i, 2)
            yield 3
            order = (0, -1, 1, 2)
            for dm in order:
                for ab in range(2):
                    for i, d in enumerate(steps):
                        s = 7 + i * 8 + i * 4 + dm % 4
                        got(ab, piece(ab, -d, i, dm), s, second(ab, -d))
                        put(ab, piece(ab, -d, i, dm), 23 + i * 4 + dm % 4, second(ab, d))
            for i, d in enumerate(steps):
                for ab in range(2):
                    for dm in order:
                        got(ab, piece(ab, -d, 1 - i, dm), 7 + i * 8 + (1 - i) * 4 + dm % 4, second(ab, -d))
                yield 5 + i
            for ab in range(2):
                for i, d in enumerate(steps):
                    for dm in order:
                        got(ab, piece(ab, 2, i, dm), 23 + i * 4 + dm % 4, second(ab, -d))
            yield 7

        def gather_chosen(par):
            ss, sr = cs.at[par], cr.at[par]

            def move(ab, at, s, dev):
                send(at, at, ss.at[ab, s], sr.at[ab, s], dev)

            def got(ab, at, s, dev):
                arrived(at, ss.at[ab, s], sr.at[ab, s], dev)

            for ab in range(2):
                k, m = place[ab]
                for i, d in enumerate(steps):
                    move(ab, chosen.at[par, ab, k, m], i, first(ab, d))
            yield 0
            for ab in range(2):
                k, m = place[ab]
                for i, d in enumerate(steps):
                    at = chosen.at[par, ab, k, (m - d + 4) % 4]
                    got(ab, at, i, first(ab, -d))
                    move(ab, chosen.at[par, ab, k, (m - d + 4) % 4, i], 2 + i, first(ab, d))
            yield 1
            for ab in range(2):
                k, m = place[ab]
                for i, d in enumerate(steps):
                    got(ab, chosen.at[par, ab, k, (m + 2) % 4, i], 2 + i, first(ab, -d))
                for i, d in enumerate(steps):
                    move(ab, chosen.at[par, ab, k], 4 + i, second(ab, d))
            yield 2
            for ab in range(2):
                k, m = place[ab]
                for i, d in enumerate(steps):
                    kk = (k - d + 4) % 4
                    got(ab, chosen.at[par, ab, kk], 4 + i, second(ab, -d))
                    move(ab, chosen.at[par, ab, kk, pl.ds(2 * i, 2)], 6 + i, second(ab, d))
            yield 3
            for ab in range(2):
                k, m = place[ab]
                for i, d in enumerate(steps):
                    got(ab, chosen.at[par, ab, (k + 2) % 4, pl.ds(2 * i, 2)], 6 + i, second(ab, -d))
            yield 4

        def until(task, mark):
            while next(task) != mark:
                pass

        def encode(d):
            ky, kx = (y + d + 4) % 4, (x + d + 4) % 4

            def tile(n, carry):
                cols = pl.ds(pl.multiple_of(n * 256, 256), 256)
                lhs = jnp.concatenate(
                    [cent[0, ky].reshape(128, D), cent[1, kx].reshape(128, D)], axis=0)
                before = jnp.dot(lhs, w_vm[:, cols], preferred_element_type=F32) + eb_ref[:, cols]
                made = jnp.maximum(before, 0.0).astype(BF16)
                pcodes[pl.ds(pl.multiple_of(ky * 128, 128), 128), cols] = made[:128]
                pcodes[pl.ds(pl.multiple_of(512 + kx * 128, 128), 128), cols] = made[128:]
                return carry

            lax.fori_loop(0, 4, tile, 0)

        rows = gather_rows(None if c == 0 else lambda: pl.semaphore_wait(go, 1))
        until(rows, 3)
        w_copy.wait()
        encode(0)
        until(rows, 5)
        encode(-1)
        until(rows, 6)
        encode(1)
        until(rows, 7)
        if c == 0:
            pl.semaphore_signal(go, inc=1, device_id=twin, device_id_type=MESH)
        encode(2)

        def rep_of(d, core_):
            return ((h + d + 4) % 4) * 2 + core_

        def chunk(rep, q):
            return codes.at[rep, :, pl.ds(q * CHUNK, CHUNK), :]

        up, down = (rep_of(1, c), w), (rep_of(-1, c), w)

        def along_z(q):
            send(chunk(r, q), chunk(r, q), zs.at[0, q], zr.at[0, q], up)
            p = (q + 2) % 4
            send(chunk(r, p), chunk(r, p), zs.at[1, p], zr.at[1, p], down)

        def pick(i, carry):
            q = (i % 2) * 2 + i // 2
            at = pl.ds(pl.multiple_of(q * CHUNK, CHUNK), CHUNK)
            place_of = pos_ref[at, :]
            lane = lax.broadcasted_iota(jnp.int32, (CHUNK, 128), 1)
            hot = jnp.concatenate(
                [(place_of == lane + 128 * n).astype(F32) for n in range(8)], axis=1).astype(BF16)
            for half in range(2):
                got = jnp.dot(hot, pcodes[:, half * HALF:(half + 1) * HALF], preferred_element_type=F32)
                codes[r, half, at, :] = got.astype(BF16)
            return carry

        lax.fori_loop(0, 2, pick, 0)
        along_z(0)
        lax.fori_loop(2, 4, pick, 0)

        def to_twin(k, q):
            part = chunk(rep_of((0, -1, 1, 2)[k], c), q)
            send(part, part, ks.at[k, q], kr.at[k, q], twin)

        def twin_arrived(k):
            for q in range(4):
                arrived(chunk(rep_of((0, -1, 1, 2)[k], 1 - c), q), ks.at[k, q], kr.at[k, q], twin)

        def pass_on(q):
            got = chunk(rep_of(-1, c), q)
            arrived(got, zs.at[0, q], zr.at[0, q], down)
            if q < 2:
                send(got, got, fs.at[0, q], fr.at[0, q], up)
            to_twin(1, q)
            p = (q + 2) % 4
            got = chunk(rep_of(1, c), p)
            arrived(got, zs.at[1, p], zr.at[1, p], up)
            if q < 2:
                send(got, got, fs.at[1, q], fr.at[1, q], down)
            to_twin(2, p)

        def far_codes():
            for q in range(2):
                arrived(chunk(rep_of(2, c), q), fs.at[0, q], fr.at[0, q], down)
                to_twin(3, q)
                arrived(chunk(rep_of(2, c), q + 2), fs.at[1, q], fr.at[1, q], up)
                to_twin(3, q + 2)

        def owner(k, p):
            return rows_ref[k] * 2 + p

        def route():
            for i in range(1, 4):
                yy = (y + i) % 4
                part = codes.at[r, :, pl.ds(pl.multiple_of(yy * CHUNK, CHUNK), CHUNK), :]
                send(part, ybuf.at[y], ys.at[i], yr.at[i], (r, wide_of(zl, yy, x)))
            mine = pltpu.make_async_copy(
                codes.at[r, :, pl.ds(pl.multiple_of(y * CHUNK, CHUNK), CHUNK), :], ybuf.at[y], l_sem)
            mine.start()
            yield 0
            mine.wait()
            for i in range(1, 4):
                src = (y - i + 4) % 4
                arrived(ybuf.at[src], ys.at[i], yr.at[i], (r, wide_of(zl, src, x)))
            for k in range(2):
                xsend[k] = ybuf[(owner(k, x % 2) // 4) % 4]
            for i in range(1, 4):
                xx = (x + i) % 4
                part = xsend.at[:, :, pl.ds(pl.multiple_of(xx * PIECE, PIECE), PIECE), :]
                send(part, xbuf.at[x], xs.at[i], xr.at[i], (r, wide_of(zl, y, xx)))
            xbuf[x] = xsend[:, :, pl.ds(pl.multiple_of(x * PIECE, PIECE), PIECE), :]
            yield 1
            for i in range(1, 4):
                src = (x - i + 4) % 4
                arrived(xbuf.at[src], xs.at[i], xr.at[i], (r, wide_of(zl, y, src)))
            for hd in range(4):
                k, p = hd // 2, hd % 2
                xo = owner(k, p) % 4
                zsend[hd] = xbuf[xo, k, :, :, pl.ds(pl.multiple_of((1 - zl) * 256, 256), 256)]
                zbuf[zl, hd] = xbuf[xo, k, :, :, pl.ds(pl.multiple_of(zl * 256, 256), 256)]
            send(zsend, zbuf.at[zl], qs, qr, other)
            yield 2
            arrived(zbuf.at[1 - zl], qs, qr, other)
            ab = h // 2
            place_k = jnp.where(ab == 0, y, x)
            place_m = jnp.where(ab == 0, x, y)
            dst = chosen.at[c, ab, place_k, place_m, zl, h % 2]
            for i in (4, 3, 5, 2, 6, 1, 7, 0):
                rd = (r + i) % 8
                hd, cd = rd // 2, (c + i) % 2
                sel[i] = zbuf[owner(hd // 2, hd % 2) // 16, hd, cd]
                if i == 0:
                    dst[...] = sel[i]
                else:
                    send(sel.at[i], dst, rs.at[0, i], rr.at[0, i], (rd, w))
                send(sel.at[i], dst, rs.at[1, i], rr.at[1, i], (rd, other[1]))
            yield 3

        def pieces_arrived(par):
            for i in range(8):
                if (c - i) % 2 != par:
                    continue
                src = (r - i + 8) % 8
                hs = src // 2
                ab = hs // 2
                at = (par, ab, jnp.where(ab == 0, y, x), jnp.where(ab == 0, x, y))
                if i > 0:
                    arrived(chosen.at[at + (zl, hs % 2)], rs.at[0, i], rr.at[0, i], (src, w))
                arrived(chosen.at[at + (1 - zl, hs % 2)], rs.at[1, i], rr.at[1, i], (src, other[1]))

        def gram(d, par, first=False):
            hs = (h + d + 4) % 4
            ab, slot = hs // 2, hs % 2
            rep = hs * 2 + par

            def quarter(qc, carry):
                parts = []
                for t in range(16):
                    k = jnp.where(ab == 0, t // 4, t % 4)
                    m = jnp.where(ab == 0, t % 4, t // 4)
                    parts.append(chosen[par, ab, k, m, qc, slot])
                lhs = jnp.concatenate(parts, axis=0)
                at = pl.ds(pl.multiple_of(qc * 256, 256), 256)
                for half in range(2):
                    made = lax.dot_general(lhs, codes[rep, half], (((0,), (0,)), ((), ())),
                                           preferred_element_type=F32)
                    cols = slice(half * HALF, (half + 1) * HALF)
                    if first:
                        out_ref[at, cols] = made
                    else:
                        out_ref[at, cols] += made
                return carry

            lax.fori_loop(0, 2, quarter, 0)

        deal = route()
        spread = [gather_chosen(par) for par in range(2)]
        if c == 0:
            until(deal, 0)
            along_z(1)
            along_z(2)
            along_z(3)
            for q in range(4):
                to_twin(0, q)
            until(deal, 1)
            until(deal, 2)
            until(deal, 3)
            pass_on(0)
            pass_on(1)
            pieces_arrived(0)
            until(spread[0], 2)
            pass_on(2)
            pass_on(3)
            until(spread[0], 4)
            gram(0, 0, first=True)
            gram(-1, 0)
            gram(1, 0)
            pieces_arrived(1)
            until(spread[1], 2)
            far_codes()
            until(spread[1], 3)
            gram(2, 0)
            until(spread[1], 4)
            for k, d in enumerate((0, -1, 1, 2)):
                twin_arrived(k)
                gram(d, 1)
        else:
            until(deal, 0)
            for q in range(4):
                to_twin(0, q)
            pieces_arrived(0)
            until(spread[0], 1)
            until(deal, 1)
            along_z(1)
            until(spread[0], 2)
            until(deal, 2)
            until(deal, 3)
            along_z(2)
            along_z(3)
            pass_on(0)
            pass_on(1)
            until(spread[0], 4)
            twin_arrived(0)
            gram(0, 0, first=True)
            pieces_arrived(1)
            until(spread[1], 2)
            pass_on(2)
            until(spread[1], 3)
            pass_on(3)
            twin_arrived(1)
            gram(-1, 0)
            until(spread[1], 4)
            gram(0, 1)
            gram(-1, 1)
            twin_arrived(2)
            gram(1, 0)
            gram(1, 1)
            twin_arrived(3)
            gram(2, 0)
            far_codes()
            gram(2, 1)

        for d in sends:
            d.wait_send()

    @pl.when(core == 0)
    def _():
        program(0)

    @pl.when(core == 1)
    def _():
        program(1)


def local(pool, ids, block_rows, enc_weight, enc_bias, dec_bias):
    vmem = pl.BlockSpec(memory_space=pltpu.VMEM)
    smem = pl.BlockSpec(memory_space=pltpu.SMEM)
    dma = pltpu.SemaphoreType.DMA
    summed = pl.pallas_call(
        kernel,
        out_shape=jax.ShapeDtypeStruct((ROWS, PANEL), F32),
        in_specs=[vmem, vmem, smem, pl.BlockSpec(memory_space=pl.ANY), vmem, vmem],
        out_specs=vmem,
        scratch_shapes=[
            pltpu.VMEM((TOK, 128), jnp.int32),
            pltpu.VMEM((D, PANEL), BF16),
            pltpu.VMEM((2, 4, 2, 4, 16, D), BF16),
            pltpu.VMEM((1024, PANEL), BF16),
            pltpu.VMEM((8, 2, TOK, HALF), BF16),
            pltpu.VMEM((4, 2, CHUNK, HALF), BF16),
            pltpu.VMEM((2, 2, CHUNK, HALF), BF16),
            pltpu.VMEM((4, 2, 2, PIECE, HALF), BF16),
            pltpu.VMEM((4, 2, PIECE, 256), BF16),
            pltpu.VMEM((2, 4, 2, PIECE, 256), BF16),
            pltpu.VMEM((8, PIECE, 256), BF16),
            pltpu.VMEM((2, 2, 4, 4, 2, 2, PIECE, 256), BF16),
            dma, pltpu.SemaphoreType.REGULAR, dma,
            dma((2, 31)), dma((2, 31)),
            dma((2, 2, 8)), dma((2, 2, 8)),
            dma((4,)), dma((4,)),
            dma((4,)), dma((4,)),
            dma, dma,
            dma((2, 8)), dma((2, 8)),
            dma((2, 4)), dma((2, 4)),
            dma((2, 2)), dma((2, 2)),
            dma((4, 4)), dma((4, 4)),
        ],
        compiler_params=pltpu.CompilerParams(
            collective_id=0, has_side_effects=True, vmem_limit_bytes=58 * 1024 * 1024),
    )(pool, ids, block_rows, enc_weight, enc_bias.reshape(1, PANEL), dec_bias.reshape(1, D))
    return summed * (1.0 / 6144.0)


def solution(mesh):
    placed = (P(("rep", "wide"), None), P("rep"), P(), P(None, "wide"), P("wide"), P())
    return jax.shard_map(
        local, mesh=mesh, in_specs=placed, out_specs=P("rep", "wide"), check_vma=False
    )
```

```python
import jax
import jax.numpy as jnp
from jax import lax
from jax.experimental import pallas as pl
from jax.experimental.pallas import tpu as pltpu
from jax.sharding import PartitionSpec as P

BLOCK = 2048
D = 4096
TOK = 768
PANEL = 1024
HALF = 512
ROWS = 512
PIECE = 48
CHUNK = 192
MESH = pl.DeviceIdType.MESH
F32 = jnp.float32
BF16 = jnp.bfloat16


def kernel(pool_ref, ids_ref, rows_ref, w_hbm, eb_ref, db_ref, out_ref,
           hot_ref, w_vm, cent, pcodes, codes, ybuf, xsend, xbuf, zsend, zbuf, sel, chosen,
           w_sem, go, l_sem, ps, pr, cs, cr, ys, yr, xs, xr, qs, qr, rs, rr, zs, zr, fs, fr, ks, kr):
    r = lax.axis_index("rep")
    w = lax.axis_index("wide")
    h, core = r // 2, r % 2
    zl, y, x = w // 16, (w // 4) % 4, w % 4

    def wide_of(zz, yy, xx):
        return zz * 16 + yy * 4 + xx

    w_copy = pltpu.make_async_copy(w_hbm, w_vm, w_sem)
    w_copy.start()

    barrier = pltpu.get_barrier_semaphore()
    partners = [((r + i) % 8, w) for i in range(1, 8)]
    partners += [(r, wide_of(zl, (y + i) % 4, x)) for i in range(1, 4)]
    partners += [(r, wide_of(zl, y, (x + i) % 4)) for i in range(1, 4)]
    partners += [((r + i) % 8, wide_of(1 - zl, y, x)) for i in range(8)]
    for device in partners:
        pl.semaphore_signal(barrier, inc=1, device_id=device, device_id_type=MESH)

    for ab in range(2):
        values = pool_ref[ab * 16:(ab + 1) * 16, :].astype(F32)
        power = jnp.mean(values * values, axis=-1, keepdims=True)
        centered = (values * lax.rsqrt(power + 1e-06) - db_ref[...]).astype(BF16)
        if ab == 0:
            cent[0, y, zl, x] = centered
        else:
            cent[1, x, zl, y] = centered

    pl.semaphore_wait(barrier, len(partners))

    def program(c):
        sends = []
        twin = (h * 2 + 1 - c, w)
        other = (r, wide_of(1 - zl, y, x))

        def copy(src, dst, ssem, rsem, dev):
            return pltpu.make_async_remote_copy(
                src_ref=src, dst_ref=dst, send_sem=ssem, recv_sem=rsem,
                device_id=dev, device_id_type=MESH)

        def send(src, dst, ssem, rsem, dev):
            d = copy(src, dst, ssem, rsem, dev)
            d.start()
            sends.append(d)

        def arrived(dst, ssem, rsem, dev):
            copy(dst, dst, ssem, rsem, dev).wait_recv()

        place = ((y, x), (x, y))
        steps = (1, -1)

        def first(ab, d):
            if ab == 0:
                return (r, wide_of(zl, y, (x + d + 4) % 4))
            return (r, wide_of(zl, (y + d + 4) % 4, x))

        def second(ab, d):
            return first(1 - ab, d)

        def gather_rows(hold):
            def piece(ab, dk, e, dm):
                k, m = place[ab]
                return cent.at[ab, (k + dk + 4) % 4, zl if e == 0 else 1 - zl, (m + dm + 4) % 4]

            def got(ab, at, s, dev):
                arrived(at, ps.at[ab, s], pr.at[ab, s], dev)

            def put(ab, at, s, dev):
                send(at, at, ps.at[ab, s], pr.at[ab, s], dev)

            if hold is not None:
                hold()

            def across(ab, e, dm):
                for i, d in enumerate(steps):
                    put(ab, piece(ab, 0, e, dm), 7 + i * 8 + e * 4 + dm % 4, second(ab, d))

            for ab in range(2):
                put(ab, piece(ab, 0, 0, 0), 0, other)
                for i, d in enumerate(steps):
                    put(ab, piece(ab, 0, 0, 0), 1 + i * 2, first(ab, d))
                across(ab, 0, 0)
            for ab in range(2):
                got(ab, piece(ab, 0, 1, 0), 0, other)
                for i, d in enumerate(steps):
                    put(ab, piece(ab, 0, 1, 0), 2 + i * 2, first(ab, d))
                across(ab, 1, 0)
            for e in range(2):
                for i, d in ((0, 1), (1, -1)):
                    for ab in range(2):
                        got(ab, piece(ab, 0, e, -d), 1 + i * 2 + e, first(ab, -d))
                        if e == i:
                            put(ab, piece(ab, 0, e, -d), 5 + i, first(ab, d))
                        across(ab, e, -d)
            for i, d in enumerate(steps):
                for ab in range(2):
                    got(ab, piece(ab, 0, i, 2), 5 + i, first(ab, -d))
                    across(ab, i, 2)
            yield 3
            order = (0, -1, 1, 2)
            for dm in order:
                for ab in range(2):
                    for i, d in enumerate(steps):
                        s = 7 + i * 8 + i * 4 + dm % 4
                        got(ab, piece(ab, -d, i, dm), s, second(ab, -d))
                        put(ab, piece(ab, -d, i, dm), 23 + i * 4 + dm % 4, second(ab, d))
                yield 4
            for i, d in enumerate(steps):
                for ab in range(2):
                    for dm in order:
                        got(ab, piece(ab, -d, 1 - i, dm), 7 + i * 8 + (1 - i) * 4 + dm % 4, second(ab, -d))
                yield 5 + i
            for ab in range(2):
                for i, d in enumerate(steps):
                    for dm in order:
                        got(ab, piece(ab, 2, i, dm), 23 + i * 4 + dm % 4, second(ab, -d))
            yield 7

        def gather_chosen(par):
            ss, sr = cs.at[par], cr.at[par]

            def move(ab, at, s, dev):
                send(at, at, ss.at[ab, s], sr.at[ab, s], dev)

            def got(ab, at, s, dev):
                arrived(at, ss.at[ab, s], sr.at[ab, s], dev)

            for ab in range(2):
                k, m = place[ab]
                for i, d in enumerate(steps):
                    move(ab, chosen.at[par, ab, k, m], i, first(ab, d))
            yield 0
            for ab in range(2):
                k, m = place[ab]
                for i, d in enumerate(steps):
                    at = chosen.at[par, ab, k, (m - d + 4) % 4]
                    got(ab, at, i, first(ab, -d))
                    move(ab, chosen.at[par, ab, k, (m - d + 4) % 4, i], 2 + i, first(ab, d))
            yield 1
            for ab in range(2):
                k, m = place[ab]
                for i, d in enumerate(steps):
                    got(ab, chosen.at[par, ab, k, (m + 2) % 4, i], 2 + i, first(ab, -d))
                for i, d in enumerate(steps):
                    move(ab, chosen.at[par, ab, k], 4 + i, second(ab, d))
            yield 2
            for ab in range(2):
                k, m = place[ab]
                for i, d in enumerate(steps):
                    kk = (k - d + 4) % 4
                    got(ab, chosen.at[par, ab, kk], 4 + i, second(ab, -d))
                    move(ab, chosen.at[par, ab, kk, pl.ds(2 * i, 2)], 6 + i, second(ab, d))
            yield 3
            for ab in range(2):
                k, m = place[ab]
                for i, d in enumerate(steps):
                    got(ab, chosen.at[par, ab, (k + 2) % 4, pl.ds(2 * i, 2)], 6 + i, second(ab, -d))
            yield 4

        def until(task, mark):
            while next(task) != mark:
                pass

        def encode(d, tiles=(0, 4)):
            ky, kx = (y + d + 4) % 4, (x + d + 4) % 4

            def tile(n, carry):
                cols = pl.ds(pl.multiple_of(n * 256, 256), 256)
                lhs = jnp.concatenate(
                    [cent[0, ky].reshape(128, D), cent[1, kx].reshape(128, D)], axis=0)
                before = jnp.dot(lhs, w_vm[:, cols], preferred_element_type=F32) + eb_ref[:, cols]
                made = jnp.maximum(before, 0.0).astype(BF16)
                pcodes[pl.ds(pl.multiple_of(ky * 128, 128), 128), cols] = made[:128]
                pcodes[pl.ds(pl.multiple_of(512 + kx * 128, 128), 128), cols] = made[128:]
                return carry

            lax.fori_loop(*tiles, tile, 0)

        def mark(n, carry):
            at = pl.ds(pl.multiple_of(n * 128, 128), 128)
            ids = ids_ref[at].reshape(1, 128)
            ab, wp = (ids // 16) % 2, ids // 32
            z_, y_, x_ = wp // 16, (wp // 4) % 4, wp % 4
            k_ = jnp.where(ab == 0, y_, x_)
            m_ = jnp.where(ab == 0, x_, y_)
            place_of = ab * 512 + k_ * 128 + z_ * 64 + m_ * 16 + ids % 16
            place_of = jnp.broadcast_to(place_of, (128, 128)).T
            lane = lax.broadcasted_iota(jnp.int32, (128, 128), 1)
            for j in range(8):
                hot_ref[at, j * 128:(j + 1) * 128] = (place_of == lane + 128 * j).astype(F32).astype(BF16)
            return carry

        rows = gather_rows(None if c == 0 else lambda: pl.semaphore_wait(go, 1))
        until(rows, 3)
        w_copy.wait()
        for n in range(4):
            next(rows)
            encode(0, (n, n + 1))
        lax.fori_loop(0, TOK // 128, mark, 0)
        until(rows, 5)
        encode(-1)
        until(rows, 6)
        encode(1)
        until(rows, 7)
        if c == 0:
            pl.semaphore_signal(go, inc=1, device_id=twin, device_id_type=MESH)
        encode(2)

        def rep_of(d, core_):
            return ((h + d + 4) % 4) * 2 + core_

        def chunk(rep, q):
            return codes.at[rep, :, pl.ds(q * CHUNK, CHUNK), :]

        up, down = (rep_of(1, c), w), (rep_of(-1, c), w)

        def along_z(q):
            send(chunk(r, q), chunk(r, q), zs.at[0, q], zr.at[0, q], up)
            p = (q + 2) % 4
            send(chunk(r, p), chunk(r, p), zs.at[1, p], zr.at[1, p], down)

        def pick(i, carry):
            q = (i % 2) * 2 + i // 2
            at = pl.ds(pl.multiple_of(q * CHUNK, CHUNK), CHUNK)
            for half in range(2):
                got = jnp.dot(hot_ref[at, :], pcodes[:, half * HALF:(half + 1) * HALF], preferred_element_type=F32)
                codes[r, half, at, :] = got.astype(BF16)
            return carry

        lax.fori_loop(0, 2, pick, 0)
        along_z(0)
        lax.fori_loop(2, 4, pick, 0)

        def to_twin(k, q):
            part = chunk(rep_of((0, -1, 1, 2)[k], c), q)
            send(part, part, ks.at[k, q], kr.at[k, q], twin)

        def twin_arrived(k):
            for q in range(4):
                arrived(chunk(rep_of((0, -1, 1, 2)[k], 1 - c), q), ks.at[k, q], kr.at[k, q], twin)

        def pass_on(q):
            got = chunk(rep_of(-1, c), q)
            arrived(got, zs.at[0, q], zr.at[0, q], down)
            if q < 2:
                send(got, got, fs.at[0, q], fr.at[0, q], up)
            to_twin(1, q)
            p = (q + 2) % 4
            got = chunk(rep_of(1, c), p)
            arrived(got, zs.at[1, p], zr.at[1, p], up)
            if q < 2:
                send(got, got, fs.at[1, q], fr.at[1, q], down)
            to_twin(2, p)

        def far_codes():
            for q in range(2):
                arrived(chunk(rep_of(2, c), q), fs.at[0, q], fr.at[0, q], down)
                to_twin(3, q)
                arrived(chunk(rep_of(2, c), q + 2), fs.at[1, q], fr.at[1, q], up)
                to_twin(3, q + 2)

        def owner(k, p):
            return rows_ref[k] * 2 + p

        def route():
            for i in range(1, 4):
                yy = (y + i) % 4
                part = codes.at[r, :, pl.ds(pl.multiple_of(yy * CHUNK, CHUNK), CHUNK), :]
                send(part, ybuf.at[y], ys.at[i], yr.at[i], (r, wide_of(zl, yy, x)))
            mine = pltpu.make_async_copy(
                codes.at[r, :, pl.ds(pl.multiple_of(y * CHUNK, CHUNK), CHUNK), :], ybuf.at[y], l_sem)
            mine.start()
            yield 0
            mine.wait()
            for i in range(1, 4):
                src = (y - i + 4) % 4
                arrived(ybuf.at[src], ys.at[i], yr.at[i], (r, wide_of(zl, src, x)))
            for k in range(2):
                xsend[k] = ybuf[(owner(k, x % 2) // 4) % 4]
            for i in range(1, 4):
                xx = (x + i) % 4
                part = xsend.at[:, :, pl.ds(pl.multiple_of(xx * PIECE, PIECE), PIECE), :]
                send(part, xbuf.at[x], xs.at[i], xr.at[i], (r, wide_of(zl, y, xx)))
            xbuf[x] = xsend[:, :, pl.ds(pl.multiple_of(x * PIECE, PIECE), PIECE), :]
            yield 1
            for i in range(1, 4):
                src = (x - i + 4) % 4
                arrived(xbuf.at[src], xs.at[i], xr.at[i], (r, wide_of(zl, y, src)))
            for hd in range(4):
                k, p = hd // 2, hd % 2
                xo = owner(k, p) % 4
                zsend[hd] = xbuf[xo, k, :, :, pl.ds(pl.multiple_of((1 - zl) * 256, 256), 256)]
                zbuf[zl, hd] = xbuf[xo, k, :, :, pl.ds(pl.multiple_of(zl * 256, 256), 256)]
            send(zsend, zbuf.at[zl], qs, qr, other)
            yield 2
            arrived(zbuf.at[1 - zl], qs, qr, other)
            ab = h // 2
            place_k = jnp.where(ab == 0, y, x)
            place_m = jnp.where(ab == 0, x, y)
            dst = chosen.at[c, ab, place_k, place_m, zl, h % 2]
            for i in (4, 3, 5, 2, 6, 1, 7, 0):
                rd = (r + i) % 8
                hd, cd = rd // 2, (c + i) % 2
                sel[i] = zbuf[owner(hd // 2, hd % 2) // 16, hd, cd]
                if i == 0:
                    dst[...] = sel[i]
                else:
                    send(sel.at[i], dst, rs.at[0, i], rr.at[0, i], (rd, w))
                send(sel.at[i], dst, rs.at[1, i], rr.at[1, i], (rd, other[1]))
            yield 3

        def pieces_arrived(par):
            for i in range(8):
                if (c - i) % 2 != par:
                    continue
                src = (r - i + 8) % 8
                hs = src // 2
                ab = hs // 2
                at = (par, ab, jnp.where(ab == 0, y, x), jnp.where(ab == 0, x, y))
                if i > 0:
                    arrived(chosen.at[at + (zl, hs % 2)], rs.at[0, i], rr.at[0, i], (src, w))
                arrived(chosen.at[at + (1 - zl, hs % 2)], rs.at[1, i], rr.at[1, i], (src, other[1]))

        def gram(d, par, first=False):
            hs = (h + d + 4) % 4
            ab, slot = hs // 2, hs % 2
            rep = hs * 2 + par

            def quarter(qc, carry):
                parts = []
                for t in range(16):
                    k = jnp.where(ab == 0, t // 4, t % 4)
                    m = jnp.where(ab == 0, t % 4, t // 4)
                    parts.append(chosen[par, ab, k, m, qc, slot])
                lhs = jnp.concatenate(parts, axis=0)
                at = pl.ds(pl.multiple_of(qc * 256, 256), 256)
                for half in range(2):
                    made = lax.dot_general(lhs, codes[rep, half], (((0,), (0,)), ((), ())),
                                           preferred_element_type=F32)
                    cols = slice(half * HALF, (half + 1) * HALF)
                    if first:
                        out_ref[at, cols] = made
                    else:
                        out_ref[at, cols] += made
                return carry

            lax.fori_loop(0, 2, quarter, 0)

        deal = route()
        spread = [gather_chosen(par) for par in range(2)]
        if c == 0:
            until(deal, 0)
            along_z(1)
            along_z(2)
            along_z(3)
            for q in range(4):
                to_twin(0, q)
            until(deal, 1)
            until(deal, 2)
            until(deal, 3)
            pass_on(0)
            pieces_arrived(0)
            until(spread[0], 2)
            pass_on(1)
            pass_on(2)
            pass_on(3)
            until(spread[0], 4)
            gram(0, 0, first=True)
            gram(-1, 0)
            gram(1, 0)
            pieces_arrived(1)
            until(spread[1], 2)
            far_codes()
            until(spread[1], 3)
            gram(2, 0)
            until(spread[1], 4)
            for k, d in enumerate((0, -1, 1, 2)):
                twin_arrived(k)
                gram(d, 1)
        else:
            until(deal, 0)
            for q in range(4):
                to_twin(0, q)
            until(deal, 1)
            along_z(1)
            until(deal, 2)
            pieces_arrived(0)
            until(spread[0], 1)
            until(deal, 3)
            along_z(2)
            along_z(3)
            until(spread[0], 2)
            pass_on(0)
            until(spread[0], 3)
            pass_on(1)
            until(spread[0], 4)
            twin_arrived(0)
            gram(0, 0, first=True)
            pieces_arrived(1)
            until(spread[1], 2)
            pass_on(2)
            until(spread[1], 3)
            pass_on(3)
            twin_arrived(1)
            gram(-1, 0)
            until(spread[1], 4)
            gram(0, 1)
            gram(-1, 1)
            twin_arrived(2)
            gram(1, 0)
            gram(1, 1)
            twin_arrived(3)
            gram(2, 0)
            far_codes()
            gram(2, 1)

        for d in sends:
            d.wait_send()

    @pl.when(core == 0)
    def _():
        program(0)

    @pl.when(core == 1)
    def _():
        program(1)


def local(pool, ids, block_rows, enc_weight, enc_bias, dec_bias):
    vmem = pl.BlockSpec(memory_space=pltpu.VMEM)
    smem = pl.BlockSpec(memory_space=pltpu.SMEM)
    dma = pltpu.SemaphoreType.DMA
    summed = pl.pallas_call(
        kernel,
        out_shape=jax.ShapeDtypeStruct((ROWS, PANEL), F32),
        in_specs=[vmem, vmem, smem, pl.BlockSpec(memory_space=pl.ANY), vmem, vmem],
        out_specs=vmem,
        scratch_shapes=[
            pltpu.VMEM((TOK, 1024), BF16),
            pltpu.VMEM((D, PANEL), BF16),
            pltpu.VMEM((2, 4, 2, 4, 16, D), BF16),
            pltpu.VMEM((1024, PANEL), BF16),
            pltpu.VMEM((8, 2, TOK, HALF), BF16),
            pltpu.VMEM((4, 2, CHUNK, HALF), BF16),
            pltpu.VMEM((2, 2, CHUNK, HALF), BF16),
            pltpu.VMEM((4, 2, 2, PIECE, HALF), BF16),
            pltpu.VMEM((4, 2, PIECE, 256), BF16),
            pltpu.VMEM((2, 4, 2, PIECE, 256), BF16),
            pltpu.VMEM((8, PIECE, 256), BF16),
            pltpu.VMEM((2, 2, 4, 4, 2, 2, PIECE, 256), BF16),
            dma, pltpu.SemaphoreType.REGULAR, dma,
            dma((2, 31)), dma((2, 31)),
            dma((2, 2, 8)), dma((2, 2, 8)),
            dma((4,)), dma((4,)),
            dma((4,)), dma((4,)),
            dma, dma,
            dma((2, 8)), dma((2, 8)),
            dma((2, 4)), dma((2, 4)),
            dma((2, 2)), dma((2, 2)),
            dma((4, 4)), dma((4, 4)),
        ],
        compiler_params=pltpu.CompilerParams(
            collective_id=0, has_side_effects=True, vmem_limit_bytes=58 * 1024 * 1024),
    )(pool, ids, block_rows, enc_weight, enc_bias.reshape(1, PANEL), dec_bias.reshape(1, D))
    return summed * (1.0 / 6144.0)


def solution(mesh):
    placed = (P(("rep", "wide"), None), P("rep"), P(), P(None, "wide"), P("wide"), P())
    return jax.shard_map(
        local, mesh=mesh, in_specs=placed, out_specs=P("rep", "wide"), check_vma=False
    )
```

```python
import jax
import jax.numpy as jnp
from jax import lax
from jax.experimental import pallas as pl
from jax.experimental.pallas import tpu as pltpu
from jax.sharding import PartitionSpec as P

BLOCK = 2048
D = 4096
TOK = 768
PANEL = 1024
HALF = 512
ROWS = 512
PIECE = 48
CHUNK = 192
MESH = pl.DeviceIdType.MESH
F32 = jnp.float32
BF16 = jnp.bfloat16


def kernel(pool_ref, ids_ref, rows_ref, w_hbm, eb_ref, db_ref, out_ref,
           hot_ref, w_vm, cent, pcodes, codes, ybuf, xsend, xbuf, zsend, zbuf, sel, chosen,
           w_sem, go, l_sem, ps, pr, cs, cr, ys, yr, xs, xr, qs, qr, rs, rr, zs, zr, fs, fr, ks, kr):
    r = lax.axis_index("rep")
    w = lax.axis_index("wide")
    h, core = r // 2, r % 2
    zl, y, x = w // 16, (w // 4) % 4, w % 4

    def wide_of(zz, yy, xx):
        return zz * 16 + yy * 4 + xx

    w_copy = pltpu.make_async_copy(w_hbm, w_vm, w_sem)
    w_copy.start()

    barrier = pltpu.get_barrier_semaphore()
    partners = [((r + i) % 8, w) for i in range(1, 8)]
    partners += [(r, wide_of(zl, (y + i) % 4, x)) for i in range(1, 4)]
    partners += [(r, wide_of(zl, y, (x + i) % 4)) for i in range(1, 4)]
    partners += [((r + i) % 8, wide_of(1 - zl, y, x)) for i in range(8)]
    for device in partners:
        pl.semaphore_signal(barrier, inc=1, device_id=device, device_id_type=MESH)

    for ab in range(2):
        values = pool_ref[ab * 16:(ab + 1) * 16, :].astype(F32)
        power = jnp.mean(values * values, axis=-1, keepdims=True)
        centered = (values * lax.rsqrt(power + 1e-06) - db_ref[...]).astype(BF16)
        if ab == 0:
            cent[0, y, zl, x] = centered
        else:
            cent[1, x, zl, y] = centered

    pl.semaphore_wait(barrier, len(partners))

    def program(c):
        sends = []
        twin = (h * 2 + 1 - c, w)
        other = (r, wide_of(1 - zl, y, x))

        def copy(src, dst, ssem, rsem, dev):
            return pltpu.make_async_remote_copy(
                src_ref=src, dst_ref=dst, send_sem=ssem, recv_sem=rsem,
                device_id=dev, device_id_type=MESH)

        def send(src, dst, ssem, rsem, dev):
            d = copy(src, dst, ssem, rsem, dev)
            d.start()
            sends.append(d)

        def arrived(dst, ssem, rsem, dev):
            copy(dst, dst, ssem, rsem, dev).wait_recv()

        place = ((y, x), (x, y))
        steps = (1, -1)

        def first(ab, d):
            if ab == 0:
                return (r, wide_of(zl, y, (x + d + 4) % 4))
            return (r, wide_of(zl, (y + d + 4) % 4, x))

        def second(ab, d):
            return first(1 - ab, d)

        def gather_rows(hold):
            def piece(ab, dk, e, dm):
                k, m = place[ab]
                return cent.at[ab, (k + dk + 4) % 4, zl if e == 0 else 1 - zl, (m + dm + 4) % 4]

            def got(ab, at, s, dev):
                arrived(at, ps.at[ab, s], pr.at[ab, s], dev)

            def put(ab, at, s, dev):
                send(at, at, ps.at[ab, s], pr.at[ab, s], dev)

            if hold is not None:
                hold()

            def across(ab, e, dm):
                for i, d in enumerate(steps):
                    put(ab, piece(ab, 0, e, dm), 7 + i * 8 + e * 4 + dm % 4, second(ab, d))

            for ab in range(2):
                put(ab, piece(ab, 0, 0, 0), 0, other)
                for i, d in enumerate(steps):
                    put(ab, piece(ab, 0, 0, 0), 1 + i * 2, first(ab, d))
                across(ab, 0, 0)
            for ab in range(2):
                got(ab, piece(ab, 0, 1, 0), 0, other)
                for i, d in enumerate(steps):
                    put(ab, piece(ab, 0, 1, 0), 2 + i * 2, first(ab, d))
                across(ab, 1, 0)
            for e in range(2):
                for i, d in ((0, 1), (1, -1)):
                    for ab in range(2):
                        got(ab, piece(ab, 0, e, -d), 1 + i * 2 + e, first(ab, -d))
                        if e == i:
                            put(ab, piece(ab, 0, e, -d), 5 + i, first(ab, d))
                        across(ab, e, -d)
            for i, d in enumerate(steps):
                for ab in range(2):
                    got(ab, piece(ab, 0, i, 2), 5 + i, first(ab, -d))
                    across(ab, i, 2)
            yield 3
            order = (0, -1, 1, 2)
            for dm in order:
                for ab in range(2):
                    for i, d in enumerate(steps):
                        s = 7 + i * 8 + i * 4 + dm % 4
                        got(ab, piece(ab, -d, i, dm), s, second(ab, -d))
                        put(ab, piece(ab, -d, i, dm), 23 + i * 4 + dm % 4, second(ab, d))
                yield 4
            for i, d in enumerate(steps):
                for ab in range(2):
                    for dm in order:
                        got(ab, piece(ab, -d, 1 - i, dm), 7 + i * 8 + (1 - i) * 4 + dm % 4, second(ab, -d))
                yield 5 + i
            for ab in range(2):
                for i, d in enumerate(steps):
                    for dm in order:
                        got(ab, piece(ab, 2, i, dm), 23 + i * 4 + dm % 4, second(ab, -d))
            yield 7

        def gather_chosen(par):
            ss, sr = cs.at[par], cr.at[par]

            def move(ab, at, s, dev):
                send(at, at, ss.at[ab, s], sr.at[ab, s], dev)

            def got(ab, at, s, dev):
                arrived(at, ss.at[ab, s], sr.at[ab, s], dev)

            for ab in range(2):
                k, m = place[ab]
                for i, d in enumerate(steps):
                    move(ab, chosen.at[par, ab, k, m], i, first(ab, d))
            yield 0
            for ab in range(2):
                k, m = place[ab]
                for i, d in enumerate(steps):
                    at = chosen.at[par, ab, k, (m - d + 4) % 4]
                    got(ab, at, i, first(ab, -d))
                    move(ab, chosen.at[par, ab, k, (m - d + 4) % 4, i], 2 + i, first(ab, d))
            yield 1
            for ab in range(2):
                k, m = place[ab]
                for i, d in enumerate(steps):
                    got(ab, chosen.at[par, ab, k, (m + 2) % 4, i], 2 + i, first(ab, -d))
                for i, d in enumerate(steps):
                    move(ab, chosen.at[par, ab, k], 4 + i, second(ab, d))
            yield 2
            for ab in range(2):
                k, m = place[ab]
                for i, d in enumerate(steps):
                    kk = (k - d + 4) % 4
                    got(ab, chosen.at[par, ab, kk], 4 + i, second(ab, -d))
                    move(ab, chosen.at[par, ab, kk, pl.ds(2 * i, 2)], 6 + i, second(ab, d))
            yield 3
            for ab in range(2):
                k, m = place[ab]
                for i, d in enumerate(steps):
                    got(ab, chosen.at[par, ab, (k + 2) % 4, pl.ds(2 * i, 2)], 6 + i, second(ab, -d))
            yield 4

        def until(task, mark):
            while next(task) != mark:
                pass

        def encode(d, tiles=(0, 4)):
            ky, kx = (y + d + 4) % 4, (x + d + 4) % 4

            def tile(n, carry):
                cols = pl.ds(pl.multiple_of(n * 256, 256), 256)
                lhs = jnp.concatenate(
                    [cent[0, ky].reshape(128, D), cent[1, kx].reshape(128, D)], axis=0)
                before = jnp.dot(lhs, w_vm[:, cols], preferred_element_type=F32) + eb_ref[:, cols]
                made = jnp.maximum(before, 0.0).astype(BF16)
                pcodes[pl.ds(pl.multiple_of(ky * 128, 128), 128), cols] = made[:128]
                pcodes[pl.ds(pl.multiple_of(512 + kx * 128, 128), 128), cols] = made[128:]
                return carry

            lax.fori_loop(*tiles, tile, 0)

        def mark(n, carry):
            at = pl.ds(pl.multiple_of(n * 128, 128), 128)
            ids = ids_ref[at].reshape(1, 128)
            ab, wp = (ids // 16) % 2, ids // 32
            z_, y_, x_ = wp // 16, (wp // 4) % 4, wp % 4
            k_ = jnp.where(ab == 0, y_, x_)
            m_ = jnp.where(ab == 0, x_, y_)
            place_of = ab * 512 + k_ * 128 + z_ * 64 + m_ * 16 + ids % 16
            place_of = jnp.broadcast_to(place_of, (128, 128)).T
            lane = lax.broadcasted_iota(jnp.int32, (128, 128), 1)
            for j in range(8):
                hot_ref[at, j * 128:(j + 1) * 128] = (place_of == lane + 128 * j).astype(F32).astype(BF16)
            return carry

        rows = gather_rows(None if c == 0 else lambda: pl.semaphore_wait(go, 1))
        until(rows, 3)
        w_copy.wait()
        for n in range(4):
            next(rows)
            encode(0, (n, n + 1))
        lax.fori_loop(0, TOK // 128, mark, 0)
        until(rows, 5)
        encode(-1)
        until(rows, 6)
        encode(1)
        until(rows, 7)
        if c == 0:
            pl.semaphore_signal(go, inc=1, device_id=twin, device_id_type=MESH)
        encode(2)

        def rep_of(d, core_):
            return ((h + d + 4) % 4) * 2 + core_

        def chunk(rep, q):
            return codes.at[rep, :, pl.ds(q * CHUNK, CHUNK), :]

        up, down = (rep_of(1, c), w), (rep_of(-1, c), w)

        def along_z(q):
            send(chunk(r, q), chunk(r, q), zs.at[0, q], zr.at[0, q], up)
            p = (q + 2) % 4
            send(chunk(r, p), chunk(r, p), zs.at[1, p], zr.at[1, p], down)

        def pick(i, carry):
            q = (i % 2) * 2 + i // 2
            at = pl.ds(pl.multiple_of(q * CHUNK, CHUNK), CHUNK)
            for half in range(2):
                got = jnp.dot(hot_ref[at, :], pcodes[:, half * HALF:(half + 1) * HALF], preferred_element_type=F32)
                codes[r, half, at, :] = got.astype(BF16)
            return carry

        lax.fori_loop(0, 2, pick, 0)
        along_z(0)
        lax.fori_loop(2, 4, pick, 0)

        def to_twin(k, q):
            part = chunk(rep_of((0, -1, 1, 2)[k], c), q)
            send(part, part, ks.at[k, q], kr.at[k, q], twin)

        def twin_arrived(k, chunks=(0, 1, 2, 3)):
            for q in chunks:
                arrived(chunk(rep_of((0, -1, 1, 2)[k], 1 - c), q), ks.at[k, q], kr.at[k, q], twin)

        def pass_on(q):
            got = chunk(rep_of(-1, c), q)
            arrived(got, zs.at[0, q], zr.at[0, q], down)
            if q < 2:
                send(got, got, fs.at[0, q], fr.at[0, q], up)
            to_twin(1, q)
            p = (q + 2) % 4
            got = chunk(rep_of(1, c), p)
            arrived(got, zs.at[1, p], zr.at[1, p], up)
            if q < 2:
                send(got, got, fs.at[1, q], fr.at[1, q], down)
            to_twin(2, p)

        def far_codes(pairs=(0, 1)):
            for q in pairs:
                arrived(chunk(rep_of(2, c), q), fs.at[0, q], fr.at[0, q], down)
                to_twin(3, q)
                arrived(chunk(rep_of(2, c), q + 2), fs.at[1, q], fr.at[1, q], up)
                to_twin(3, q + 2)

        def owner(k, p):
            return rows_ref[k] * 2 + p

        def route():
            for i in range(1, 4):
                yy = (y + i) % 4
                part = codes.at[r, :, pl.ds(pl.multiple_of(yy * CHUNK, CHUNK), CHUNK), :]
                send(part, ybuf.at[y], ys.at[i], yr.at[i], (r, wide_of(zl, yy, x)))
            mine = pltpu.make_async_copy(
                codes.at[r, :, pl.ds(pl.multiple_of(y * CHUNK, CHUNK), CHUNK), :], ybuf.at[y], l_sem)
            mine.start()
            yield 0
            mine.wait()
            for i in range(1, 4):
                src = (y - i + 4) % 4
                arrived(ybuf.at[src], ys.at[i], yr.at[i], (r, wide_of(zl, src, x)))
            for k in range(2):
                xsend[k] = ybuf[(owner(k, x % 2) // 4) % 4]
            for i in range(1, 4):
                xx = (x + i) % 4
                part = xsend.at[:, :, pl.ds(pl.multiple_of(xx * PIECE, PIECE), PIECE), :]
                send(part, xbuf.at[x], xs.at[i], xr.at[i], (r, wide_of(zl, y, xx)))
            xbuf[x] = xsend[:, :, pl.ds(pl.multiple_of(x * PIECE, PIECE), PIECE), :]
            yield 1
            for i in range(1, 4):
                src = (x - i + 4) % 4
                arrived(xbuf.at[src], xs.at[i], xr.at[i], (r, wide_of(zl, y, src)))
            for hd in range(4):
                k, p = hd // 2, hd % 2
                xo = owner(k, p) % 4
                zsend[hd] = xbuf[xo, k, :, :, pl.ds(pl.multiple_of((1 - zl) * 256, 256), 256)]
                zbuf[zl, hd] = xbuf[xo, k, :, :, pl.ds(pl.multiple_of(zl * 256, 256), 256)]
            send(zsend, zbuf.at[zl], qs, qr, other)
            yield 2
            arrived(zbuf.at[1 - zl], qs, qr, other)
            ab = h // 2
            place_k = jnp.where(ab == 0, y, x)
            place_m = jnp.where(ab == 0, x, y)
            dst = chosen.at[c, ab, place_k, place_m, zl, h % 2]
            for i in (4, 3, 5, 2, 6, 1, 7, 0):
                rd = (r + i) % 8
                hd, cd = rd // 2, (c + i) % 2
                sel[i] = zbuf[owner(hd // 2, hd % 2) // 16, hd, cd]
                if i == 0:
                    dst[...] = sel[i]
                else:
                    send(sel.at[i], dst, rs.at[0, i], rr.at[0, i], (rd, w))
                send(sel.at[i], dst, rs.at[1, i], rr.at[1, i], (rd, other[1]))
            yield 3

        def pieces_arrived(par):
            for i in range(8):
                if (c - i) % 2 != par:
                    continue
                src = (r - i + 8) % 8
                hs = src // 2
                ab = hs // 2
                at = (par, ab, jnp.where(ab == 0, y, x), jnp.where(ab == 0, x, y))
                if i > 0:
                    arrived(chosen.at[at + (zl, hs % 2)], rs.at[0, i], rr.at[0, i], (src, w))
                arrived(chosen.at[at + (1 - zl, hs % 2)], rs.at[1, i], rr.at[1, i], (src, other[1]))

        def gram(d, par, first=False, chunks=(0, 1, 2, 3)):
            hs = (h + d + 4) % 4
            ab, slot = hs // 2, hs % 2
            rep = hs * 2 + par

            def quarter(qc, carry):
                parts = []
                for t in [4 * q + n for q in chunks for n in range(4)]:
                    k = jnp.where(ab == 0, t // 4, t % 4)
                    m = jnp.where(ab == 0, t % 4, t // 4)
                    parts.append(chosen[par, ab, k, m, qc, slot])
                lhs = jnp.concatenate(parts, axis=0)
                at = pl.ds(pl.multiple_of(qc * 256, 256), 256)
                for half in range(2):
                    rhs = jnp.concatenate(
                        [codes[rep, half, q * CHUNK:(q + 1) * CHUNK, :] for q in chunks], axis=0)
                    made = lax.dot_general(lhs, rhs, (((0,), (0,)), ((), ())),
                                           preferred_element_type=F32)
                    cols = slice(half * HALF, (half + 1) * HALF)
                    if first:
                        out_ref[at, cols] = made
                    else:
                        out_ref[at, cols] += made
                return carry

            lax.fori_loop(0, 2, quarter, 0)

        deal = route()
        spread = [gather_chosen(par) for par in range(2)]
        if c == 0:
            until(deal, 0)
            along_z(1)
            along_z(2)
            along_z(3)
            for q in range(4):
                to_twin(0, q)
            until(deal, 1)
            until(deal, 2)
            until(deal, 3)
            pass_on(0)
            pieces_arrived(0)
            until(spread[0], 2)
            pass_on(1)
            pass_on(2)
            pass_on(3)
            until(spread[0], 4)
            gram(0, 0, first=True)
            gram(-1, 0)
            gram(1, 0)
            pieces_arrived(1)
            until(spread[1], 2)
            far_codes()
            until(spread[1], 3)
            gram(2, 0)
            until(spread[1], 4)
            for k, d in enumerate((0, -1, 1)):
                twin_arrived(k)
                gram(d, 1)
            for pair in ((0, 2), (1, 3)):
                twin_arrived(3, pair)
                gram(2, 1, chunks=pair)
        else:
            until(deal, 0)
            for q in range(4):
                to_twin(0, q)
            until(deal, 1)
            along_z(1)
            until(deal, 2)
            pieces_arrived(0)
            until(spread[0], 1)
            until(deal, 3)
            along_z(2)
            along_z(3)
            until(spread[0], 2)
            pass_on(0)
            until(spread[0], 3)
            pass_on(1)
            until(spread[0], 4)
            twin_arrived(0)
            gram(0, 0, first=True)
            pieces_arrived(1)
            until(spread[1], 2)
            pass_on(2)
            until(spread[1], 3)
            pass_on(3)
            twin_arrived(1)
            gram(-1, 0)
            until(spread[1], 4)
            gram(0, 1)
            gram(-1, 1)
            twin_arrived(2)
            gram(1, 0)
            gram(1, 1)
            twin_arrived(3)
            gram(2, 0)
            far_codes((0,))
            gram(2, 1, chunks=(0, 2))
            far_codes((1,))
            gram(2, 1, chunks=(1, 3))

        for d in sends:
            d.wait_send()

    @pl.when(core == 0)
    def _():
        program(0)

    @pl.when(core == 1)
    def _():
        program(1)


def local(pool, ids, block_rows, enc_weight, enc_bias, dec_bias):
    vmem = pl.BlockSpec(memory_space=pltpu.VMEM)
    smem = pl.BlockSpec(memory_space=pltpu.SMEM)
    dma = pltpu.SemaphoreType.DMA
    summed = pl.pallas_call(
        kernel,
        out_shape=jax.ShapeDtypeStruct((ROWS, PANEL), F32),
        in_specs=[vmem, vmem, smem, pl.BlockSpec(memory_space=pl.ANY), vmem, vmem],
        out_specs=vmem,
        scratch_shapes=[
            pltpu.VMEM((TOK, 1024), BF16),
            pltpu.VMEM((D, PANEL), BF16),
            pltpu.VMEM((2, 4, 2, 4, 16, D), BF16),
            pltpu.VMEM((1024, PANEL), BF16),
            pltpu.VMEM((8, 2, TOK, HALF), BF16),
            pltpu.VMEM((4, 2, CHUNK, HALF), BF16),
            pltpu.VMEM((2, 2, CHUNK, HALF), BF16),
            pltpu.VMEM((4, 2, 2, PIECE, HALF), BF16),
            pltpu.VMEM((4, 2, PIECE, 256), BF16),
            pltpu.VMEM((2, 4, 2, PIECE, 256), BF16),
            pltpu.VMEM((8, PIECE, 256), BF16),
            pltpu.VMEM((2, 2, 4, 4, 2, 2, PIECE, 256), BF16),
            dma, pltpu.SemaphoreType.REGULAR, dma,
            dma((2, 31)), dma((2, 31)),
            dma((2, 2, 8)), dma((2, 2, 8)),
            dma((4,)), dma((4,)),
            dma((4,)), dma((4,)),
            dma, dma,
            dma((2, 8)), dma((2, 8)),
            dma((2, 4)), dma((2, 4)),
            dma((2, 2)), dma((2, 2)),
            dma((4, 4)), dma((4, 4)),
        ],
        compiler_params=pltpu.CompilerParams(
            collective_id=0, has_side_effects=True, vmem_limit_bytes=58 * 1024 * 1024),
    )(pool, ids, block_rows, enc_weight, enc_bias.reshape(1, PANEL), dec_bias.reshape(1, D))
    return summed * (1.0 / 6144.0)


def solution(mesh):
    placed = (P(("rep", "wide"), None), P("rep"), P(), P(None, "wide"), P("wide"), P())
    return jax.shard_map(
        local, mesh=mesh, in_specs=placed, out_specs=P("rep", "wide"), check_vma=False
    )
```
